256 devices in a mesh: head: 32 (over y, x, core), blk: 8 (over z).
Axes of the slice: x: 4, y: 4, z: 8, core: 2. Of those that a mesh axis runs over, the one named last changes fastest.
Arguments:
- queries: bfloat16 [6144, 4096], P('blk', 'head'), may hold values from -10 to 10
- key_rows: bfloat16 [6144, 1024], P('blk', 'head'), may hold values from -10 to 10
- value_rows: bfloat16 [6144, 1024], P('blk', 'head'), may hold values from -4 to 4
- out_grad: bfloat16 [6144, 4096], P('blk', 'head'), may hold values from -1.5 to 1.5
- doc_lengths: int32 [16], replicated, may hold values from 1 to 1536, 6144 in all
Outputs:
- query_grad: bfloat16 [6144, 4096], P('blk', 'head')
- key_grad: bfloat16 [6144, 1024], P('blk', 'head')
- value_grad: bfloat16 [6144, 1024], P('blk', 'head')
The draws below stay inside these ranges and needn't reach their ends.
Inputs may be any that keep to these rules, and one draw needn't show every extreme that they name: `doc_lengths`: they sum to 6144; the longest is exactly 1536.
All inputs are finite; a program needn't handle non-finite values.
Results may differ from the reference program's by a relative error of at most 0.0071.
Values may be sent and summed in bfloat16 or wider, within the bound.
A program may use at most 64 MiB of HBM per device.

```python
import math
import jax
import jax.numpy as jnp
import numpy as np
from jax import lax

HD = 128
GROUP = 4
H = 32
KVH = 8
TOKENS = 6144
MAXDOC = 1536
NDOCS = 16


def draw_queries(key, part):
    key = jax.random.fold_in(key, 11)
    result = jax.random.truncated_normal(key, -4.0, 4.0, (TOKENS, H, HD))
    return result.reshape(TOKENS, H * HD).astype(jnp.bfloat16)


def draw_key_rows(key, part):
    key = jax.random.fold_in(key, 12)
    result = jax.random.truncated_normal(key, -4.0, 4.0, (TOKENS, KVH, HD))
    return result.reshape(TOKENS, KVH * HD).astype(jnp.bfloat16)


def steps_of(stream_key, dims, pieces, low, high):
    loudness, own = 1.0, jax.random.fold_in(stream_key, 6)
    for dim, shards_of in pieces:
        steps = jnp.exp(jax.random.uniform(jax.random.fold_in(own, dim), (shards_of,), jnp.float32, low / len(pieces), high / len(pieces)))
        loudness = loudness * jnp.repeat(steps, dims[dim] // shards_of).reshape([-1 if axis == dim else 1 for axis in range(len(dims))])
    return loudness


def length_profile(count, total, limit, slope):
    weights = [(1 << 20) // math.isqrt(grade ** slope) + 1 for grade in range(2, count + 1)]
    spare, given = total - limit - (count - 1), [1] * (count - 1)
    while spare > 0:
        free = [i for i in range(count - 1) if given[i] < limit]
        whole, remaining = sum([weights[i] for i in free]), spare
        for i in free:
            addition = min(limit - given[i], max(1, remaining * weights[i] // whole), spare)
            given[i] = given[i] + addition
            spare = spare - addition
    return np.array([limit] + given)


def uneven_parts(key, number_of, total, most, lean):
    if number_of == 2:
        one = jax.random.randint(key, (), max(1, total - most), min(most, total - 1) + 1)
        return jnp.stack([one, total - one])
    tallies = jnp.asarray(length_profile(number_of, total, most, lean), jnp.int32)
    twos = (number_of - 1) // 2
    giver, receiver = tallies[1:1 + 2 * twos:2], tallies[2:2 + 2 * twos:2]
    room = jnp.minimum(giver - 1, most - receiver)
    passed = jax.random.randint(jax.random.fold_in(key, 1), (twos,), 0, 1 << 20) % (room + 1)
    tallies = tallies.at[1:1 + 2 * twos:2].set(giver - passed).at[2:2 + 2 * twos:2].set(receiver + passed)
    return tallies[jax.random.permutation(jax.random.fold_in(key, 2), number_of)]


def scatter_about(rng, extent, scale, limit, cuts=(), kind=jnp.bfloat16):
    factor_of = steps_of(rng, extent, cuts, -0.22, 0.18) if cuts else 1.0
    entries = jax.random.normal(rng, extent, jnp.float32) * scale * factor_of
    return jnp.minimum(jnp.maximum(entries, -limit), limit).astype(kind)


def setup_inputs(seed: int = 0) -> dict:
    arg_keys = jax.random.split(jax.random.key(seed), 6)
    queries = draw_queries(jax.random.fold_in(arg_keys[5], 71), 0)
    key_rows = draw_key_rows(jax.random.fold_in(arg_keys[5], 71), 0)
    value_rows = scatter_about(arg_keys[2], (TOKENS, KVH * HD), 1.0, 4.0, ((0, 8), (1, 32)))
    out_grad = scatter_about(arg_keys[3], (TOKENS, H * HD), 0.25, 1.5, ((0, 8), (1, 32)))
    doc_lengths = uneven_parts(arg_keys[4], NDOCS, TOKENS, MAXDOC, 2).astype(jnp.int32)
    return {"queries": queries, "key_rows": key_rows, "value_rows": value_rows, "out_grad": out_grad, "doc_lengths": doc_lengths}


def document_ids(doc_lengths, span_rows):
    doc_ends = jnp.cumsum(doc_lengths).astype(jnp.int32)
    positions = jnp.arange(span_rows, dtype=jnp.int32)
    return jnp.sum((doc_ends[None, :] <= positions[:, None]).astype(jnp.int32), axis=1)


def reference(queries, key_rows, value_rows, out_grad, doc_lengths):
    doc_ids = document_ids(doc_lengths, TOKENS)
    positions = jnp.arange(TOKENS, dtype=jnp.int32)
    allowed = (positions[None, :] <= positions[:, None]) & (doc_ids[None, :] == doc_ids[:, None])
    softmax_scale = HD ** -0.5
    query_heads = queries.reshape(TOKENS, H, HD).transpose(1, 0, 2)
    grad_heads = out_grad.reshape(TOKENS, H, HD).transpose(1, 0, 2)
    key_heads = key_rows.reshape(TOKENS, KVH, HD).transpose(1, 0, 2)
    value_heads = value_rows.reshape(TOKENS, KVH, HD).transpose(1, 0, 2)

    def one_head(head_index):
        kv_group = head_index // GROUP
        head_queries = query_heads[head_index]
        head_grad = grad_heads[head_index]
        key_tile = key_heads[kv_group]
        value_tile = value_heads[kv_group]
        scores = jnp.dot(head_queries, key_tile.T, preferred_element_type=jnp.float32) * softmax_scale
        masked = jnp.where(allowed, scores, -jnp.inf)
        row_max = jnp.max(masked, axis=1, keepdims=True)
        log_norm = row_max + jnp.log(jnp.sum(jnp.exp(masked - row_max), axis=1, keepdims=True))
        weights = jnp.exp(jnp.where(allowed, scores - log_norm, -jnp.inf))
        attended = jnp.dot(weights, value_tile.astype(jnp.float32), precision=lax.Precision.HIGHEST)
        row_delta = jnp.sum(head_grad.astype(jnp.float32) * attended, axis=1, keepdims=True)
        weights_b = weights.astype(jnp.bfloat16)
        prob_grad = jnp.dot(head_grad, value_tile.T, preferred_element_type=jnp.float32)
        score_grad = (weights * (prob_grad - row_delta)).astype(jnp.bfloat16)
        query_part = (jnp.dot(score_grad, key_tile, preferred_element_type=jnp.float32) * softmax_scale).astype(jnp.bfloat16)
        key_part = jnp.dot(score_grad.T, head_queries, preferred_element_type=jnp.float32)
        value_part = jnp.dot(weights_b.T, head_grad, preferred_element_type=jnp.float32)
        return query_part, key_part, value_part

    query_parts, key_parts, value_parts = lax.map(one_head, jnp.arange(H, dtype=jnp.int32))
    query_grad = query_parts.transpose(1, 0, 2).reshape(TOKENS, H * HD)
    key_sum = jnp.sum(key_parts.reshape(KVH, GROUP, TOKENS, HD), axis=1) * softmax_scale
    value_sum = jnp.sum(value_parts.reshape(KVH, GROUP, TOKENS, HD), axis=1)
    key_grad = key_sum.astype(jnp.bfloat16).transpose(1, 0, 2).reshape(TOKENS, KVH * HD)
    value_grad = value_sum.astype(jnp.bfloat16).transpose(1, 0, 2).reshape(TOKENS, KVH * HD)
    return query_grad, key_grad, value_grad
```

```python
import functools

import jax
import jax.numpy as jnp
from jax import lax
from jax.experimental import pallas as pl
from jax.experimental.pallas import tpu as pltpu
from jax.sharding import PartitionSpec as P

f32, bf16 = jnp.float32, jnp.bfloat16
MESH = pl.DeviceIdType.MESH
LOG2E = 1.4426950408889634
BIG = 65536.0
SLOTS = 3


def dot(a, b):
    return jnp.dot(a, b, preferred_element_type=f32)


def dot_nt(a, b):
    return lax.dot_general(a, b, (((1,), (1,)), ((), ())), preferred_element_type=f32)


def kernel(
    blocks,
    doc_ref, q_hbm, k_hbm, v_hbm, do_hbm,
    dq_hbm, dk_hbm, dv_hbm,
    kv_in, qp, dop, kvt, p_s, ds_s, o_s, m_s, g_s, qst, dost, part, dq, dq_out, kv_out,
    pst, prc, xst, xrc, zst, zrc,
    load_sem, store_sem,
    z_send, z_recv, x_send, x_recv, p_send, p_recv, f_send, f_recv,
    rz_send, rz_recv, rx_send, rx_recv, rp_send, rp_recv,
):
    R, D = q_hbm.shape
    W = k_hbm.shape[1]
    T = R // 3
    scale = D ** -0.5
    C = scale * LOG2E
    head = lax.axis_index("head")
    blk = lax.axis_index("blk")
    core = lax.rem(head, 2)
    side = lax.rem(head // 2, 2)
    partner = {"head": head + 1 - 2 * core}
    across = {"head": head + 2 - 4 * side}
    up = {"blk": lax.rem(blk + 1, blocks)}
    down = {"blk": lax.rem(blk + blocks - 1, blocks)}
    q0 = 2 * side + core
    q1 = 2 * side + 1 - core
    q2 = 2 * (1 - side) + core
    q3 = 2 * (1 - side) + 1 - core

    def quarter(i):
        return pl.ds(pl.multiple_of(W * i, W), W)

    def remote(src, dst, send, recv, device):
        return pltpu.make_async_remote_copy(
            src_ref=src, dst_ref=dst, send_sem=send, recv_sem=recv,
            device_id=device, device_id_type=MESH,
        )

    barrier = pltpu.get_barrier_semaphore()
    for device in (partner, across, up, down):
        pl.semaphore_signal(barrier, inc=1, device_id=device, device_id_type=MESH)
    loads = [
        pltpu.make_async_copy(src, dst, load_sem.at[i])
        for i, (src, dst) in enumerate((
            (k_hbm, kv_in.at[0]), (v_hbm, kv_in.at[1]),
            (q_hbm, qp.at[:, 0:D]), (do_hbm, dop.at[:, 0:D]),
        ))
    ]
    for load in loads:
        load.start()
    for kv in range(2):
        loads[kv].wait()
        kvt[0, kv, quarter(q0), :] = kv_in[kv].astype(f32).T.astype(bf16)
    pl.semaphore_wait(barrier, 4)

    def rows(s, kv, i):
        return kvt.at[s, kv, quarter(i), :]

    def send_z(s, kv):
        return remote(rows(s, kv, q0), rows(s + 1, kv, q0), z_send.at[s, kv], z_recv.at[s, kv], up)

    def send_x(s, kv):
        return remote(rows(s, kv, q0), rows(s, kv, q0), x_send.at[s, kv], x_recv.at[s, kv], across)

    def send_p(s, kv):
        return remote(rows(s, kv, q0), rows(s, kv, q0), p_send.at[s, kv], p_recv.at[s, kv], partner)

    def send_f(s, kv):
        return remote(rows(s, kv, q2), rows(s, kv, q2), f_send.at[s, kv], f_recv.at[s, kv], partner)

    def landed(ref, sem):
        pltpu.make_async_copy(ref, ref, sem).wait()

    def spread(s, kv):
        if s < SLOTS - 1:
            send_z(s, kv).start()
        send_x(s, kv).start()
        send_p(s, kv).start()

    def pass_on(s):
        for kv in range(2):
            landed(rows(s, kv, q2), x_recv.at[s, kv])
            send_f(s, kv).start()

    def arrive(s):
        for kv in range(2):
            landed(rows(s, kv, q0), z_recv.at[s - 1, kv])
            spread(s, kv)

    def complete(s):
        for kv in range(2):
            landed(rows(s, kv, q1), p_recv.at[s, kv])
            landed(rows(s, kv, q3), f_recv.at[s, kv])

    for kv in range(2):
        spread(0, kv)

    starts, ends, total = [], [], jnp.int32(0)
    docs = doc_ref.shape[0]
    for n in range(docs):
        starts.append(total)
        total = total + doc_ref[n]
        ends.append(total)

    def bounds(shape, dim):
        n_of = lax.broadcasted_iota(jnp.int32, shape, dim)
        first = jnp.zeros(shape, jnp.int32)
        last = jnp.zeros(shape, jnp.int32)
        for n in range(docs):
            first = jnp.where(n_of == n, starts[n], first)
            last = jnp.where(n_of == n, ends[n], last)
        return first, last

    first, last = bounds((1, D), 1)
    pos = blk * R + lax.broadcasted_iota(jnp.int32, (R, D), 0)
    qp[:, D:] = jnp.where((pos >= first) & (pos < last), 1.0, 0.0).astype(bf16)
    first, last = bounds((docs, D), 0)
    first = jnp.concatenate([first] * (R // D), axis=1)
    last = jnp.concatenate([last] * (R // D), axis=1)
    for s in range(SLOTS):
        pos = lax.rem(blk + blocks - s, blocks) * R + lax.broadcasted_iota(jnp.int32, (docs, R), 1)
        kvt[s, 0, D:D + docs, :] = jnp.where((pos >= first) & (pos < last), 0.0, -BIG).astype(bf16)
        kvt[s, 0, D + docs:, :] = jnp.zeros((D - docs, R), bf16)
        kvt[s, 1, D:, :] = jnp.ones((D, R), bf16)

    def key_range(s, rt):
        return {0: (0, (rt + 1) * T), 1: (0, R), 2: (rt * T, R)}[s]

    def row_range(s, kt):
        return {0: (kt * T, R), 1: (0, R), 2: (0, (kt + 1) * T)}[s]

    def forward(s, rt):
        k0, k1 = key_range(s, rt)
        at = slice(rt * T, (rt + 1) * T)
        scores = dot(qp[at, :], kvt[s, 0, :, k0:k1])
        if s == 0:
            keep = lax.broadcasted_iota(jnp.int32, (T, T), 0) >= lax.broadcasted_iota(jnp.int32, (T, T), 1)
            diagonal = jnp.where(keep, scores[:, k1 - k0 - T:], -BIG)
            scores = diagonal if rt == 0 else jnp.concatenate([scores[:, :k1 - k0 - T], diagonal], axis=1)
        top = jnp.max(scores, axis=1, keepdims=True)
        weights = jnp.exp2((scores - top) * C).astype(bf16)
        p_s[s, at, k0:k1] = weights
        o_s[s, at, :] = dot_nt(weights, kvt[s, 1, :, k0:k1])
        m_s[s, at, :] = jnp.broadcast_to(top, (T, D))

    def combine(rt):
        at = slice(rt * T, (rt + 1) * T)
        tops = [m_s[s, at, :] for s in range(SLOTS)]
        top = functools.reduce(jnp.maximum, tops)
        factors = [jnp.exp2((x - top) * C) for x in tops]
        attended = sum(factors[s] * o_s[s, at, :D] for s in range(SLOTS))
        norm = sum(factors[s] * o_s[s, at, D:] for s in range(SLOTS))
        inverse = 1.0 / norm
        grad = dop[at, :D].astype(f32)
        query = qp[at, :D].astype(f32)
        left = -(jnp.sum(grad * attended, axis=1, keepdims=True) * inverse)
        lane = lax.broadcasted_iota(jnp.int32, (T, D), 1)
        terms = jnp.zeros((T, D), f32)
        for i in range(3):
            term = left.astype(bf16).astype(f32)
            left = left - term
            terms = jnp.where(lane == i, term, terms)
        dop[at, D:] = terms.astype(bf16)
        for s in range(SLOTS):
            factor = factors[s] * inverse
            g_s[s, at, :] = factor
            qst[s, :, at] = (query * factor).T.astype(bf16)
            dost[s, :, at] = (grad * factor).T.astype(bf16)

    def backward(s, kt):
        r0, r1 = row_range(s, kt)
        at = slice(kt * T, (kt + 1) * T)
        prob_grad = dot(dop[r0:r1, :], kvt[s, 1, :, at])
        weights = p_s[s, r0:r1, at]
        score_grad = (weights.astype(f32) * prob_grad).astype(bf16)
        ds_s[r0:r1, at] = score_grad
        part[s, 0, :, at] = dot(qst[s, :, r0:r1], score_grad)
        part[s, 1, :, at] = dot(dost[s, :, r0:r1], weights)

    def query_part(s, rt):
        k0, k1 = key_range(s, rt)
        at = slice(rt * T, (rt + 1) * T)
        x = dot_nt(ds_s[at, k0:k1], kvt[s, 0, :D, k0:k1]) * g_s[s, at, :]
        if s < SLOTS - 1:
            x = dq[at, :] + x
        if s == 0:
            dq_out[at, :] = (x * scale).astype(bf16)
        else:
            dq[at, :] = x

    def reduce_p(s, kv):
        return remote(pst.at[s, kv], prc.at[s, kv], rp_send.at[s, kv], rp_recv.at[s, kv], partner)

    def reduce_x(s, kv):
        return remote(xst.at[s, kv], xrc.at[s, kv], rx_send.at[s, kv], rx_recv.at[s, kv], across)

    def reduce_z(s, kv):
        return remote(zst.at[s - 1, kv], zrc.at[s - 1, kv], rz_send.at[s - 1, kv], rz_recv.at[s - 1, kv], down)

    def to_partner(s):
        for kv in range(2):
            for j in range(2):
                pst[s, kv, j] = part[s, kv, quarter(2 * j + 1 - core), :].astype(bf16)
            reduce_p(s, kv).start()

    def to_across(s):
        for kv in range(2):
            reduce_p(s, kv).wait_recv()
            xst[s, kv] = (part[s, kv, quarter(q2), :] + prc[s, kv, 1 - side].astype(f32)).astype(bf16)
            reduce_x(s, kv).start()

    def summed(s, kv):
        reduce_x(s, kv).wait_recv()
        total = part[s, kv, quarter(q0), :] + prc[s, kv, side].astype(f32) + xrc[s, kv].astype(f32)
        if s < SLOTS - 1:
            reduce_z(s + 1, kv).wait_recv()
            total = total + zrc[s, kv].astype(f32)
        return total

    def to_down(s):
        for kv in range(2):
            zst[s - 1, kv] = summed(s, kv).astype(bf16)
            reduce_z(s, kv).start()

    pass_on(0)
    arrive(1)
    for load in loads[2:]:
        load.wait()
    complete(0)
    for rt in range(3):
        forward(0, rt)
    pass_on(1)
    arrive(2)
    complete(1)
    for rt in range(3):
        forward(1, rt)
    pass_on(2)
    complete(2)
    for rt in range(3):
        forward(2, rt)
    for rt in range(3):
        combine(rt)

    for kt in range(3):
        backward(2, kt)
    to_partner(2)
    for rt in range(3):
        query_part(2, rt)
    backward(1, 0)
    to_across(2)
    backward(1, 1)
    backward(1, 2)
    to_partner(1)
    to_down(2)
    for rt in range(3):
        query_part(1, rt)
    backward(0, 0)
    to_across(1)
    backward(0, 1)
    backward(0, 2)
    to_partner(0)
    for rt in range(3):
        query_part(0, rt)
    dq_store = pltpu.make_async_copy(dq_out, dq_hbm, store_sem.at[2])
    dq_store.start()
    to_down(1)
    to_across(0)
    stores = [
        pltpu.make_async_copy(kv_out.at[kv], (dk_hbm, dv_hbm)[kv], store_sem.at[kv]) for kv in range(2)
    ]
    for kv in range(2):
        total = summed(0, kv)
        kv_out[kv] = ((total * scale) if kv == 0 else total).T.astype(bf16)
        stores[kv].start()

    for kv in range(2):
        for s in range(SLOTS):
            send_x(s, kv).wait_send()
            send_p(s, kv).wait_send()
            send_f(s, kv).wait_send()
            reduce_p(s, kv).wait_send()
            reduce_x(s, kv).wait_send()
        for s in range(SLOTS - 1):
            send_z(s, kv).wait_send()
            reduce_z(s + 1, kv).wait_send()
    for store in stores:
        store.wait()
    dq_store.wait()


def solution(mesh):
    blocks = mesh.shape["blk"]

    def shards(queries, key_rows, value_rows, out_grad, doc_lengths):
        R, D = queries.shape
        W = key_rows.shape[1]
        S = SLOTS
        hbm = pl.BlockSpec(memory_space=pl.ANY)
        vmem = pltpu.VMEM
        dma = pltpu.SemaphoreType.DMA
        flops = 2 * 6 * R * (7 * R // 3) * D
        return pl.pallas_call(
            functools.partial(kernel, blocks),
            out_shape=(
                jax.ShapeDtypeStruct((R, D), bf16),
                jax.ShapeDtypeStruct((R, W), bf16),
                jax.ShapeDtypeStruct((R, W), bf16),
            ),
            in_specs=[pl.BlockSpec(memory_space=pltpu.SMEM), hbm, hbm, hbm, hbm],
            out_specs=(hbm, hbm, hbm),
            scratch_shapes=[
                vmem((2, R, W), bf16), vmem((R, 2 * D), bf16), vmem((R, 2 * D), bf16),
                vmem((S, 2, 2 * D, R), bf16), vmem((S, R, R), bf16), vmem((R, R), bf16),
                vmem((S, R, 2 * D), f32), vmem((S, R, D), f32), vmem((S, R, D), f32),
                vmem((S, D, R), bf16), vmem((S, D, R), bf16), vmem((S, 2, D, R), f32),
                vmem((R, D), f32), vmem((R, D), bf16), vmem((2, R, W), bf16),
                vmem((S, 2, 2, W, R), bf16), vmem((S, 2, 2, W, R), bf16),
                vmem((S, 2, W, R), bf16), vmem((S, 2, W, R), bf16),
                vmem((S - 1, 2, W, R), bf16), vmem((S - 1, 2, W, R), bf16),
                dma((4,)), dma((3,)),
                dma((S - 1, 2)), dma((S - 1, 2)), dma((S, 2)), dma((S, 2)),
                dma((S, 2)), dma((S, 2)), dma((S, 2)), dma((S, 2)),
                dma((S - 1, 2)), dma((S - 1, 2)), dma((S, 2)), dma((S, 2)), dma((S, 2)), dma((S, 2)),
            ],
            compiler_params=pltpu.CompilerParams(
                collective_id=0, has_side_effects=True, vmem_limit_bytes=48 * 2**20,
            ),
            cost_estimate=pl.CostEstimate(flops=flops, bytes_accessed=4 * R * D * 2, transcendentals=R * R * 3),
        )(doc_lengths, queries, key_rows, value_rows, out_grad)

    specs = (P("blk", "head"),) * 4 + (P(),)
    return jax.shard_map(shards, mesh=mesh, in_specs=specs, out_specs=specs[:3], check_vma=False)
```

```python
import functools

import jax
import jax.numpy as jnp
from jax import lax
from jax.experimental import pallas as pl
from jax.experimental.pallas import tpu as pltpu
from jax.sharding import PartitionSpec as P

f32, bf16 = jnp.float32, jnp.bfloat16
MESH = pl.DeviceIdType.MESH
LOG2E = 1.4426950408889634
BIG = 65536.0
CHUNKS = 2
SLOTS = 3


def dot(a, b):
    return jnp.dot(a, b, preferred_element_type=f32)


def dot_nt(a, b):
    return lax.dot_general(a, b, (((1,), (1,)), ((), ())), preferred_element_type=f32)


def kernel(
    blocks,
    doc_ref, q_hbm, k_hbm, v_hbm, do_hbm,
    dq_hbm, dk_hbm, dv_hbm,
    qp, dop, kvt, p_s, ds_s, o_s, l_s, m_s, g_s, qst, dost, part, dq, dq_out, kv_out,
    pst, prc, xst, xrc, zst, zrc,
    load_sem, store_sem,
    z_send, z_recv, d_send, d_recv, x_send, x_recv, p_send, p_recv, f_send, f_recv,
    rz_send, rz_recv, rd_send, rd_recv, rx_send, rx_recv, rp_send, rp_recv,
):
    R, D = q_hbm.shape
    W = k_hbm.shape[0]
    T = R // 3
    scale = D ** -0.5
    C = scale * LOG2E
    head = lax.axis_index("head")
    blk = lax.axis_index("blk")
    core = lax.rem(head, 2)
    side = lax.rem(head // 2, 2)
    partner = {"head": head + 1 - 2 * core}
    across = {"head": head + 2 - 4 * side}
    up = {"blk": lax.rem(blk + 1, blocks)}
    down = {"blk": lax.rem(blk + blocks - 1, blocks)}
    across_up, across_down = {**across, **up}, {**across, **down}
    q0 = 2 * side + core
    q1 = 2 * side + 1 - core
    q2 = 2 * (1 - side) + core
    q3 = 2 * (1 - side) + 1 - core

    def quarter(i):
        return pl.ds(pl.multiple_of(W * i, W), W)

    def chunk(c):
        return slice(c * (R // CHUNKS), (c + 1) * (R // CHUNKS))

    def tile(t):
        return slice(t * T, (t + 1) * T)

    def remote(src, dst, send, recv, device):
        return pltpu.make_async_remote_copy(
            src_ref=src, dst_ref=dst, send_sem=send, recv_sem=recv,
            device_id=device, device_id_type=MESH,
        )

    barrier = pltpu.get_barrier_semaphore()
    for device in (partner, across, up, down, across_up, across_down):
        pl.semaphore_signal(barrier, inc=1, device_id=device, device_id_type=MESH)
    kv_hbm = (k_hbm, v_hbm)
    loads = [
        pltpu.make_async_copy(src, dst, load_sem.at[i])
        for i, (src, dst) in enumerate((
            (k_hbm, kvt.at[0, 0, quarter(q0), :]), (v_hbm, kvt.at[0, 1, quarter(q0), :]),
            (q_hbm, qp.at[:, 0:D]), (do_hbm, dop.at[:, 0:D]),
        ))
    ]
    for load in loads:
        load.start()
    for load in loads[:2]:
        load.wait()
    pl.semaphore_wait(barrier, 6)

    def rows(s, kv, i, c):
        return kvt.at[s, kv, quarter(i), chunk(c)]

    def send_z(s, kv, c):
        return remote(rows(s, kv, q0, c), rows(s + 1, kv, q0, c), z_send, z_recv.at[s, kv, c], up)

    def send_d(kv, c):
        return remote(rows(1, kv, q0, c), rows(2, kv, q0, c), d_send, d_recv.at[kv, c], across_up)

    def send_x(s, kv, c):
        return remote(rows(s, kv, q0, c), rows(s, kv, q0, c), x_send, x_recv.at[s, kv, c], across)

    def send_p(s, kv, c):
        return remote(rows(s, kv, q0, c), rows(s, kv, q0, c), p_send, p_recv.at[s, kv, c], partner)

    def send_f(s, kv, c):
        return remote(rows(s, kv, q2, c), rows(s, kv, q2, c), f_send, f_recv.at[s, kv, c], partner)

    def landed(ref, sem):
        pltpu.make_async_copy(ref, ref, sem).wait()

    def spread(s, kv, c):
        if s < SLOTS - 1:
            send_z(s, kv, c).start()
            send_x(s, kv, c).start()
        if s == 1:
            send_d(kv, c).start()
        send_p(s, kv, c).start()

    def arrive(s, kv):
        for c in range(CHUNKS):
            landed(rows(s, kv, q0, c), z_recv.at[s - 1, kv, c])
            spread(s, kv, c)

    def pass_on(s, kv):
        for c in range(CHUNKS):
            landed(rows(s, kv, q2, c), x_recv.at[s, kv, c] if s < 2 else d_recv.at[kv, c])
            send_f(s, kv, c).start()

    def complete(s, kv):
        for c in range(CHUNKS):
            landed(rows(s, kv, q1, c), p_recv.at[s, kv, c])
            landed(rows(s, kv, q3, c), f_recv.at[s, kv, c])

    for kv in range(2):
        for c in range(CHUNKS):
            spread(0, kv, c)

    starts, ends, total = [], [], jnp.int32(0)
    docs = doc_ref.shape[0]
    for n in range(docs):
        starts.append(total)
        total = total + doc_ref[n]
        ends.append(total)

    def bounds(shape, dim):
        n_of = lax.broadcasted_iota(jnp.int32, shape, dim)
        first = jnp.zeros(shape, jnp.int32)
        last = jnp.zeros(shape, jnp.int32)
        for n in range(docs):
            first = jnp.where(n_of == n, starts[n], first)
            last = jnp.where(n_of == n, ends[n], last)
        return first, last

    first, last = bounds((1, D), 1)
    pos = blk * R + lax.broadcasted_iota(jnp.int32, (R, D), 0)
    qp[:, D:] = jnp.where((pos >= first) & (pos < last), 1.0, 0.0).astype(bf16)
    first, last = bounds((docs, D), 0)
    first = jnp.concatenate([first] * (R // D), axis=1)
    last = jnp.concatenate([last] * (R // D), axis=1)
    for s in range(SLOTS):
        pos = lax.rem(blk + blocks - s, blocks) * R + lax.broadcasted_iota(jnp.int32, (docs, R), 1)
        kvt[s, 0, D:D + docs, :] = jnp.where((pos >= first) & (pos < last), 0.0, -BIG).astype(bf16)
        kvt[s, 0, D + docs:, :] = jnp.zeros((D - docs, R), bf16)
        kvt[s, 1, D:, :] = jnp.ones((D, R), bf16)

    def key_range(s, rt):
        return {0: (0, (rt + 1) * T), 1: (0, R), 2: (rt * T, R)}[s]

    def row_range(s, kt):
        return {0: (kt * T, R), 1: (0, R), 2: (0, (kt + 1) * T)}[s]

    def weigh(s, rt):
        k0, k1 = key_range(s, rt)
        at = tile(rt)
        scores = dot(qp[at, :], kvt[s, 0, :, k0:k1])
        if s == 0:
            keep = lax.broadcasted_iota(jnp.int32, (T, T), 0) >= lax.broadcasted_iota(jnp.int32, (T, T), 1)
            diagonal = jnp.where(keep, scores[:, k1 - k0 - T:], -BIG)
            scores = diagonal if rt == 0 else jnp.concatenate([scores[:, :k1 - k0 - T], diagonal], axis=1)
        top = jnp.max(scores, axis=1, keepdims=True)
        weights = jnp.exp2((scores - top) * C).astype(bf16)
        p_s[s, at, k0:k1] = weights
        l_s[s, at, :] = dot_nt(weights, kvt[s, 1, D:, k0:k1])
        m_s[s, at, :] = jnp.broadcast_to(top, (T, D))

    def attend(s, rt):
        k0, k1 = key_range(s, rt)
        at = tile(rt)
        o_s[s, at, :] = dot_nt(p_s[s, at, k0:k1], kvt[s, 1, :D, k0:k1])

    def normalise(rt):
        at = tile(rt)
        tops = [m_s[s, at, :] for s in range(SLOTS)]
        top = functools.reduce(jnp.maximum, tops)
        factors = [jnp.exp2((x - top) * C) for x in tops]
        inverse = 1.0 / sum(factors[s] * l_s[s, at, :] for s in range(SLOTS))
        for s in range(SLOTS):
            g_s[s, at, :] = factors[s] * inverse

    def scaled(s, rt, source, target):
        at = tile(rt)
        target[s, :, at] = (source[at, :D].astype(f32) * g_s[s, at, :]).T.astype(bf16)

    def center(rt):
        at = tile(rt)
        attended = sum(g_s[s, at, :] * o_s[s, at, :] for s in range(SLOTS))
        left = -jnp.sum(dop[at, :D].astype(f32) * attended, axis=1, keepdims=True)
        lane = lax.broadcasted_iota(jnp.int32, (T, D), 1)
        terms = jnp.zeros((T, D), f32)
        for i in range(3):
            term = left.astype(bf16).astype(f32)
            left = left - term
            terms = jnp.where(lane == i, term, terms)
        dop[at, D:] = terms.astype(bf16)

    def value_part(s, kt):
        r0, r1 = row_range(s, kt)
        part[s, 1, :, tile(kt)] = dot(dost[s, :, r0:r1], p_s[s, r0:r1, tile(kt)])

    def key_part(s, kt):
        r0, r1 = row_range(s, kt)
        prob_grad = dot(dop[r0:r1, :], kvt[s, 1, :, tile(kt)])
        score_grad = (p_s[s, r0:r1, tile(kt)].astype(f32) * prob_grad).astype(bf16)
        ds_s[s, r0:r1, tile(kt)] = score_grad
        part[s, 0, :, tile(kt)] = dot(qst[s, :, r0:r1], score_grad)

    def query_part(s, rt):
        k0, k1 = key_range(s, rt)
        at = slice(rt * T, (rt + 1) * T)
        x = dot_nt(ds_s[s, at, k0:k1], kvt[s, 0, :D, k0:k1]) * g_s[s, at, :]
        if s < SLOTS - 1:
            x = dq[at, :] + x
        if s == 0:
            dq_out[at, :] = (x * scale).astype(bf16)
        else:
            dq[at, :] = x

    def reduce_p(s, kv, t):
        return remote(pst.at[s, kv, :, :, tile(t)], prc.at[s, kv, :, :, tile(t)], rp_send, rp_recv.at[s, kv, t], partner)

    def reduce_x(s, kv, t):
        return remote(xst.at[s, kv, :, tile(t)], xrc.at[s, kv, :, tile(t)], rx_send, rx_recv.at[s, kv, t], across)

    def reduce_d(kv, t):
        return remote(xst.at[2, kv, :, tile(t)], xrc.at[2, kv, :, tile(t)], rd_send, rd_recv.at[kv, t], across_down)

    def reduce_z(s, kv, t):
        return remote(zst.at[s - 1, kv, :, tile(t)], zrc.at[s - 1, kv, :, tile(t)], rz_send, rz_recv.at[s - 1, kv, t], down)

    def to_partner(s, kv, t):
        for j in range(2):
            pst[s, kv, j, :, tile(t)] = part[s, kv, quarter(2 * j + 1 - core), tile(t)].astype(bf16)
        reduce_p(s, kv, t).start()

    def to_across(s, kv):
        for t in range(3):
            reduce_p(s, kv, t).wait_recv()
            xst[s, kv, :, tile(t)] = (
                part[s, kv, quarter(q2), tile(t)] + prc[s, kv, 1 - side, :, tile(t)].astype(f32)
            ).astype(bf16)
            reduce_x(s, kv, t).start()

    def send_home(kv):
        for t in range(3):
            reduce_p(2, kv, t).wait_recv()
            xst[2, kv, :, tile(t)] = (
                part[2, kv, quarter(q2), tile(t)] + prc[2, kv, 1 - side, :, tile(t)].astype(f32)
            ).astype(bf16)
            reduce_d(kv, t).start()
            zst[1, kv, :, tile(t)] = (
                part[2, kv, quarter(q0), tile(t)] + prc[2, kv, side, :, tile(t)].astype(f32)
            ).astype(bf16)
            reduce_z(2, kv, t).start()

    def summed(s, kv, t):
        reduce_x(s, kv, t).wait_recv()
        total = (
            part[s, kv, quarter(q0), tile(t)] + prc[s, kv, side, :, tile(t)].astype(f32)
            + xrc[s, kv, :, tile(t)].astype(f32)
        )
        if s < SLOTS - 1:
            reduce_z(s + 1, kv, t).wait_recv()
            total = total + zrc[s, kv, :, tile(t)].astype(f32)
        if s == 1:
            reduce_d(kv, t).wait_recv()
            total = total + xrc[2, kv, :, tile(t)].astype(f32)
        return total

    def to_down(s, kv):
        for t in range(3):
            zst[s - 1, kv, :, tile(t)] = summed(s, kv, t).astype(bf16)
            reduce_z(s, kv, t).start()

    def values(s):
        for t in range(3):
            value_part(s, t)
            to_partner(s, 1, t)

    def keys(s):
        for t in range(3):
            key_part(s, t)
            to_partner(s, 0, t)

    def queries(s):
        for rt in range(3):
            query_part(s, rt)

    K, V = 0, 1
    for load in loads[2:]:
        load.wait()
    arrive(1, K)
    pass_on(0, K)
    arrive(1, V)
    pass_on(0, V)
    complete(0, K)
    for rt in range(3):
        weigh(0, rt)
    complete(0, V)
    for rt in range(3):
        attend(0, rt)
    pass_on(1, K)
    pass_on(1, V)
    arrive(2, K)
    pass_on(2, K)
    complete(1, K)
    for rt in range(3):
        weigh(1, rt)
    complete(2, K)
    for rt in range(3):
        weigh(2, rt)
    arrive(2, V)
    pass_on(2, V)
    for rt in range(3):
        normalise(rt)
        scaled(2, rt, dop, dost)
    values(2)
    for rt in range(3):
        scaled(1, rt, dop, dost)
    values(1)
    complete(1, V)
    for rt in range(3):
        attend(1, rt)
    send_home(V)
    for rt in range(3):
        scaled(0, rt, dop, dost)
    values(0)
    for rt in range(3):
        scaled(2, rt, qp, qst)
    complete(2, V)
    for rt in range(3):
        attend(2, rt)
        center(rt)
    keys(2)
    to_across(1, V)
    to_across(0, V)
    for rt in range(3):
        scaled(1, rt, qp, qst)
    keys(1)
    send_home(K)
    for rt in range(3):
        scaled(0, rt, qp, qst)
    keys(0)
    to_across(1, K)
    queries(2)
    to_across(0, K)
    queries(1)
    queries(0)
    dq_store = pltpu.make_async_copy(dq_out, dq_hbm, store_sem.at[2])
    dq_store.start()
    to_down(1, V)
    to_down(1, K)
    stores = [
        pltpu.make_async_copy(kv_out.at[kv], (dk_hbm, dv_hbm)[kv], store_sem.at[kv]) for kv in range(2)
    ]
    for kv in (V, K):
        for t in range(3):
            total = summed(0, kv, t)
            kv_out[kv, :, tile(t)] = (total * scale if kv == K else total).astype(bf16)
        stores[kv].start()

    landed(kvt.at[0:2, :, 0:W, :], x_send)
    landed(kvt.at[0, :, 0:W, :], d_send)
    landed(kvt.at[:, :, 0:W, :], p_send)
    landed(kvt.at[:, :, 0:W, :], f_send)
    landed(kvt.at[0:2, :, 0:W, :], z_send)
    landed(pst, rp_send)
    landed(xst.at[0:2], rx_send)
    landed(xst.at[2], rd_send)
    landed(zst, rz_send)
    for store in stores:
        store.wait()
    dq_store.wait()


def hand_over(*refs):
    copies = [pltpu.make_async_copy(refs[i], refs[3 + i], refs[6].at[i]) for i in range(3)]
    for copy in copies:
        copy.start()
    for copy in copies:
        copy.wait()


def solution(mesh):
    blocks = mesh.shape["blk"]

    def shards(queries, key_rows, value_rows, out_grad, doc_lengths):
        R, D = queries.shape
        W = key_rows.shape[1]
        S = SLOTS
        hbm = pl.BlockSpec(memory_space=pl.ANY)
        vmem = pltpu.VMEM
        dma = pltpu.SemaphoreType.DMA
        flops = 2 * 6 * R * (7 * R // 3) * D
        shapes = (
            jax.ShapeDtypeStruct((R, D), bf16),
            jax.ShapeDtypeStruct((W, R), bf16),
            jax.ShapeDtypeStruct((W, R), bf16),
        )
        grads = pl.pallas_call(
            functools.partial(kernel, blocks),
            out_shape=tuple(vmem(x.shape, x.dtype) for x in shapes),
            in_specs=[pl.BlockSpec(memory_space=pltpu.SMEM)] + [hbm] * 4,
            out_specs=(hbm, hbm, hbm),
            scratch_shapes=[
                vmem((R, 2 * D), bf16), vmem((R, 2 * D), bf16),
                vmem((S, 2, 2 * D, R), bf16), vmem((S, R, R), bf16), vmem((S, R, R), bf16),
                vmem((S, R, D), f32), vmem((S, R, D), f32), vmem((S, R, D), f32), vmem((S, R, D), f32),
                vmem((S, D, R), bf16), vmem((S, D, R), bf16), vmem((S, 2, D, R), f32),
                vmem((R, D), f32), vmem((R, D), bf16), vmem((2, W, R), bf16),
                vmem((S, 2, 2, W, R), bf16), vmem((S, 2, 2, W, R), bf16),
                vmem((S, 2, W, R), bf16), vmem((S, 2, W, R), bf16),
                vmem((S - 1, 2, W, R), bf16), vmem((S - 1, 2, W, R), bf16),
                dma((4,)), dma((3,)),
                dma, dma((S - 1, 2, CHUNKS)), dma, dma((2, CHUNKS)), dma, dma((S - 1, 2, CHUNKS)),
                dma, dma((S, 2, CHUNKS)), dma, dma((S, 2, CHUNKS)),
                dma, dma((S - 1, 2, 3)), dma, dma((2, 3)), dma, dma((S - 1, 2, 3)), dma, dma((S, 2, 3)),
            ],
            compiler_params=pltpu.CompilerParams(
                collective_id=0, has_side_effects=True, vmem_limit_bytes=60 * 2**20,
            ),
            cost_estimate=pl.CostEstimate(flops=flops, bytes_accessed=4 * R * D * 2, transcendentals=R * R * 3),
        )(doc_lengths, queries, key_rows.T, value_rows.T, out_grad)
        query_grad, key_grad, value_grad = pl.pallas_call(
            hand_over, out_shape=shapes, in_specs=[hbm] * 3, out_specs=(hbm,) * 3, scratch_shapes=[dma((3,))],
            compiler_params=pltpu.CompilerParams(vmem_limit_bytes=2 * 2**20),
        )(*grads)
        return query_grad, key_grad.T, value_grad.T

    specs = (P("blk", "head"),) * 4 + (P(),)
    return jax.shard_map(shards, mesh=mesh, in_specs=specs, out_specs=specs[:3], check_vma=False)
```

```python
import functools

import jax
import jax.numpy as jnp
from jax import lax
from jax.experimental import pallas as pl
from jax.experimental.pallas import tpu as pltpu
from jax.sharding import PartitionSpec as P

f32, bf16 = jnp.float32, jnp.bfloat16
MESH = pl.DeviceIdType.MESH
LOG2E = 1.4426950408889634
BIG = 65536.0
PARTS = 2
PIECES = 3
SLOTS = 3


def dot(a, b):
    return jnp.dot(a, b, preferred_element_type=f32)


def dot_nt(a, b):
    return lax.dot_general(a, b, (((1,), (1,)), ((), ())), preferred_element_type=f32)


def kernel(
    blocks,
    doc_hbm, q_hbm, k_hbm, v_hbm, do_hbm,
    dq_hbm, dk_hbm, dv_hbm,
    qp, do_in, kvt, p_s, w_s, ds_s, pg_s, e_s, l_s, m_s, g_s, delta, query_t, grad_t, part, dq, dq_out, kv_out,
    pst, prc, xst, xrc, zst, zrc,
    doc_ref, load_sem, store_sem,
    z_send, z_recv, d_send, d_recv, x_send, x_recv, p_send, p_recv, f_send, f_recv,
    rz_send, rz_recv, rd_send, rd_recv, rx_send, rx_recv, rp_send, rp_recv,
):
    R, D = q_hbm.shape
    W = k_hbm.shape[0]
    T = R // 3
    scale = D ** -0.5
    C = scale * LOG2E
    head = lax.axis_index("head")
    blk = lax.axis_index("blk")
    core = lax.rem(head, 2)
    side = lax.rem(head // 2, 2)
    partner = {"head": head + 1 - 2 * core}
    across = {"head": head + 2 - 4 * side}
    up = {"blk": lax.rem(blk + 1, blocks)}
    down = {"blk": lax.rem(blk + blocks - 1, blocks)}
    across_up, across_down = {**across, **up}, {**across, **down}
    q0 = 2 * side + core
    q1 = 2 * side + 1 - core
    q2 = 2 * (1 - side) + core
    q3 = 2 * (1 - side) + 1 - core

    def quarter(i):
        return pl.ds(pl.multiple_of(W * i, W), W)

    def cut(i, n):
        return slice(i * (R // n), (i + 1) * (R // n))

    def tile(t):
        return slice(t * T, (t + 1) * T)

    def remote(src, dst, send, recv, device):
        return pltpu.make_async_remote_copy(
            src_ref=src, dst_ref=dst, send_sem=send, recv_sem=recv,
            device_id=device, device_id_type=MESH,
        )

    barrier = pltpu.get_barrier_semaphore()
    for device in (partner, across, up, down, across_up, across_down):
        pl.semaphore_signal(barrier, inc=1, device_id=device, device_id_type=MESH)
    kv_hbm = (k_hbm, v_hbm)
    loads = [
        pltpu.make_async_copy(src, dst, load_sem.at[i])
        for i, (src, dst) in enumerate((
            (k_hbm, kvt.at[0, 0, quarter(q0), :]), (v_hbm, kvt.at[0, 1, quarter(q0), :]),
            (q_hbm, qp.at[:, 0:D]), (do_hbm, do_in), (doc_hbm, doc_ref),
        ))
    ]
    for load in loads:
        load.start()
    pl.semaphore_wait(barrier, 6)

    def rows(s, kv, i, c):
        return kvt.at[s, kv, quarter(i), cut(c, PARTS)]

    def own(s, kv, c):
        return kv_hbm[kv].at[:, cut(c, PARTS)] if s == 0 else rows(s, kv, q0, c)

    def send_z(s, kv, c):
        return remote(own(s, kv, c), rows(s + 1, kv, q0, c), z_send, z_recv.at[s, kv, c], up)

    def send_d(kv, c):
        return remote(rows(1, kv, q0, c), rows(2, kv, q0, c), d_send, d_recv.at[kv, c], across_up)

    def send_x(s, kv, c):
        return remote(own(s, kv, c), rows(s, kv, q0, c), x_send, x_recv.at[s, kv, c], across)

    def send_p(s, kv, c):
        return remote(own(s, kv, c), rows(s, kv, q0, c), p_send, p_recv.at[s, kv, c], partner)

    def send_f(s, kv, c):
        return remote(rows(s, kv, q2, c), rows(s, kv, q2, c), f_send, f_recv.at[s, kv, c], partner)

    def landed(ref, sem):
        pltpu.make_async_copy(ref, ref, sem).wait()

    def spread(s, kv, c):
        if s < SLOTS - 1:
            send_z(s, kv, c).start()
            send_x(s, kv, c).start()
        if s == 1:
            send_d(kv, c).start()
        send_p(s, kv, c).start()

    def arrive(s, kv):
        for c in range(PARTS):
            landed(rows(s, kv, q0, c), z_recv.at[s - 1, kv, c])
            spread(s, kv, c)

    def pass_on(s, kv):
        for c in range(PARTS):
            landed(rows(s, kv, q2, c), x_recv.at[s, kv, c] if s < 2 else d_recv.at[kv, c])
            send_f(s, kv, c).start()

    def complete(s, kv):
        if s == 0:
            loads[kv].wait()
        for c in range(PARTS):
            landed(rows(s, kv, q1, c), p_recv.at[s, kv, c])
            landed(rows(s, kv, q3, c), f_recv.at[s, kv, c])

    for kv in range(2):
        for c in range(PARTS):
            spread(0, kv, c)

    def prepare():
        loads[4].wait()
        starts, ends, total = [], [], jnp.int32(0)
        docs = doc_ref.shape[0]
        for n in range(docs):
            starts.append(total)
            total = total + doc_ref[n]
            ends.append(total)

        def bounds(shape, dim):
            n_of = lax.broadcasted_iota(jnp.int32, shape, dim)
            first = jnp.zeros(shape, jnp.int32)
            last = jnp.zeros(shape, jnp.int32)
            for n in range(docs):
                first = jnp.where(n_of == n, starts[n], first)
                last = jnp.where(n_of == n, ends[n], last)
            return first, last

        first, last = bounds((1, D), 1)
        pos = blk * R + lax.broadcasted_iota(jnp.int32, (R, D), 0)
        qp[:, D:] = jnp.where((pos >= first) & (pos < last), 1.0, 0.0).astype(bf16)
        first, last = bounds((docs, D), 0)
        first = jnp.concatenate([first] * (R // D), axis=1)
        last = jnp.concatenate([last] * (R // D), axis=1)
        for s in range(SLOTS):
            pos = lax.rem(blk + blocks - s, blocks) * R + lax.broadcasted_iota(jnp.int32, (docs, R), 1)
            kvt[s, 0, D:D + docs, :] = jnp.where((pos >= first) & (pos < last), 0.0, -BIG).astype(bf16)
            kvt[s, 0, D + docs:, :] = jnp.zeros((D - docs, R), bf16)
        for source, target, load in ((qp, query_t, loads[2]), (do_in, grad_t, loads[3])):
            load.wait()
            for rt in range(3):
                target[:, tile(rt)] = source[tile(rt), :D].astype(f32).T.astype(bf16)

    def key_range(s, rt):
        return {0: (0, (rt + 1) * T), 1: (0, R), 2: (rt * T, R)}[s]

    def row_range(s, kt):
        return {0: (kt * T, R), 1: (0, R), 2: (0, (kt + 1) * T)}[s]

    def row_tiles(s):
        return ((slice(0, R), slice(0, R)),) if s == 1 else tuple((tile(rt), slice(*key_range(s, rt))) for rt in range(3))

    def weigh(s):
        complete(s, 0)
        for at, keys in row_tiles(s):
            scores = dot(qp[at, :], kvt[s, 0, :, keys])
            if s == 0:
                keep = lax.broadcasted_iota(jnp.int32, (T, T), 0) >= lax.broadcasted_iota(jnp.int32, (T, T), 1)
                diagonal = jnp.where(keep, scores[:, keys.stop - T:], -BIG)
                scores = diagonal if keys.stop == T else jnp.concatenate([scores[:, :keys.stop - T], diagonal], axis=1)
            top = jnp.max(scores, axis=1, keepdims=True)
            weights = jnp.exp2((scores - top) * C)
            p_s[s, at, keys] = weights.astype(bf16)
            l_s[s, at, :] = jnp.broadcast_to(jnp.sum(weights, axis=1, keepdims=True), (at.stop - at.start, D))
            m_s[s, at, :] = jnp.broadcast_to(top, (at.stop - at.start, D))

    def slope(s):
        complete(s, 1)
        for at, keys in row_tiles(s):
            prob_grad = dot(do_in[at, :], kvt[s, 1, :D, keys])
            pg_s[s, at, keys] = prob_grad
            mean = jnp.sum(p_s[s, at, keys].astype(f32) * prob_grad, axis=1, keepdims=True)
            e_s[s, at, :] = jnp.broadcast_to(mean, (at.stop - at.start, D))

    def normalise():
        tops = [m_s[s] for s in range(SLOTS)]
        top = functools.reduce(jnp.maximum, tops)
        factors = [jnp.exp2((x - top) * C) for x in tops]
        inverse = 1.0 / sum(factors[s] * l_s[s] for s in range(SLOTS))
        for s in range(SLOTS):
            g_s[s] = factors[s] * inverse

    def center():
        delta[...] = sum(g_s[s] * e_s[s] for s in range(SLOTS))

    def across_lanes(x, keys):
        return jnp.concatenate([x] * ((keys.stop - keys.start) // D), axis=1)

    def values(s):
        for at, keys in row_tiles(s):
            w_s[s, at, keys] = (p_s[s, at, keys].astype(f32) * across_lanes(g_s[s, at, :], keys)).astype(bf16)
        for kt in range(3):
            r0, r1 = row_range(s, kt)
            part[s, 1, :, tile(kt)] = dot(grad_t[:, r0:r1], w_s[s, r0:r1, tile(kt)])
        to_partner(s, 1)

    def keys(s):
        for at, keys in row_tiles(s):
            score_grad = w_s[s, at, keys].astype(f32) * (pg_s[s, at, keys] - across_lanes(delta[at, :], keys))
            ds_s[s, at, keys] = score_grad.astype(bf16)
        for kt in range(3):
            r0, r1 = row_range(s, kt)
            part[s, 0, :, tile(kt)] = dot(query_t[:, r0:r1], ds_s[s, r0:r1, tile(kt)])
        to_partner(s, 0)

    def queries(s):
        for at, keys in row_tiles(s):
            x = dot_nt(ds_s[s, at, keys], kvt[s, 0, :D, keys])
            if s < SLOTS - 1:
                x = dq[at, :] + x
            if s == 0:
                dq_out[at, :] = (x * scale).astype(bf16)
            else:
                dq[at, :] = x

    def piece(t):
        return cut(t, PIECES)

    def reduce_p(s, kv, t):
        return remote(pst.at[s, kv, :, :, piece(t)], prc.at[s, kv, :, :, piece(t)], rp_send, rp_recv.at[s, kv, t], partner)

    def reduce_x(s, kv, t):
        return remote(xst.at[s, kv, :, piece(t)], xrc.at[s, kv, :, piece(t)], rx_send, rx_recv.at[s, kv, t], across)

    def reduce_d(kv, t):
        return remote(xst.at[2, kv, :, piece(t)], xrc.at[2, kv, :, piece(t)], rd_send, rd_recv.at[kv, t], across_down)

    def reduce_z(s, kv, t):
        return remote(zst.at[s - 1, kv, :, piece(t)], zrc.at[s - 1, kv, :, piece(t)], rz_send, rz_recv.at[s - 1, kv, t], down)

    def to_partner(s, kv):
        for t in range(PIECES):
            for j in range(2):
                pst[s, kv, j, :, piece(t)] = part[s, kv, quarter(2 * j + 1 - core), piece(t)].astype(bf16)
            reduce_p(s, kv, t).start()

    def of_pair(s, kv, t, i, j):
        return part[s, kv, quarter(i), piece(t)] + prc[s, kv, j, :, piece(t)].astype(f32)

    def to_across(s, kv):
        for t in range(PIECES):
            reduce_p(s, kv, t).wait_recv()
            xst[s, kv, :, piece(t)] = of_pair(s, kv, t, q2, 1 - side).astype(bf16)
            reduce_x(s, kv, t).start()

    def send_home(kv):
        for t in range(PIECES):
            reduce_p(2, kv, t).wait_recv()
            xst[2, kv, :, piece(t)] = of_pair(2, kv, t, q2, 1 - side).astype(bf16)
            reduce_d(kv, t).start()
            zst[1, kv, :, piece(t)] = of_pair(2, kv, t, q0, side).astype(bf16)
            reduce_z(2, kv, t).start()

    def summed(s, kv, t):
        reduce_x(s, kv, t).wait_recv()
        reduce_z(s + 1, kv, t).wait_recv()
        total = of_pair(s, kv, t, q0, side) + xrc[s, kv, :, piece(t)].astype(f32) + zrc[s, kv, :, piece(t)].astype(f32)
        if s == 1:
            reduce_d(kv, t).wait_recv()
            total = total + xrc[2, kv, :, piece(t)].astype(f32)
        return total

    def to_down(kv):
        for t in range(PIECES):
            zst[0, kv, :, piece(t)] = summed(1, kv, t).astype(bf16)
            reduce_z(1, kv, t).start()

    stores = [
        pltpu.make_async_copy(src, dst, store_sem.at[i])
        for i, (src, dst) in enumerate(((kv_out.at[0], dk_hbm), (kv_out.at[1], dv_hbm), (dq_out, dq_hbm)))
    ]

    def finish(kv):
        for t in range(PIECES):
            total = summed(0, kv, t)
            kv_out[kv, :, piece(t)] = (total * scale if kv == 0 else total).astype(bf16)
        stores[kv].start()

    K, V = 0, 1
    prepare()
    for kv in (K, V):
        arrive(1, kv)
        pass_on(0, kv)
    weigh(0)
    slope(0)
    pass_on(1, K)
    pass_on(1, V)
    arrive(2, K)
    pass_on(2, K)
    weigh(1)
    weigh(2)
    arrive(2, V)
    pass_on(2, V)
    normalise()
    values(2)
    slope(1)
    values(1)
    send_home(V)
    values(0)
    slope(2)
    center()
    keys(2)
    to_across(1, V)
    to_across(0, V)
    keys(1)
    send_home(K)
    keys(0)
    to_across(1, K)
    queries(2)
    to_across(0, K)
    queries(1)
    queries(0)
    stores[2].start()
    to_down(V)
    to_down(K)
    finish(V)
    finish(K)

    landed(kvt.at[0:2, :, 0:W, :], x_send)
    landed(kvt.at[0, :, 0:W, :], d_send)
    landed(kvt.at[:, :, 0:W, :], p_send)
    landed(kvt.at[:, :, 0:W, :], f_send)
    landed(kvt.at[0:2, :, 0:W, :], z_send)
    landed(pst, rp_send)
    landed(xst.at[0:2], rx_send)
    landed(xst.at[2], rd_send)
    landed(zst, rz_send)
    for store in stores:
        store.wait()


def hand_over(*refs):
    copies = [pltpu.make_async_copy(refs[i], refs[3 + i], refs[6].at[i]) for i in range(3)]
    for copy in copies:
        copy.start()
    for copy in copies:
        copy.wait()


def solution(mesh):
    blocks = mesh.shape["blk"]

    def shards(queries, key_rows, value_rows, out_grad, doc_lengths):
        R, D = queries.shape
        W = key_rows.shape[1]
        S = SLOTS
        hbm = pl.BlockSpec(memory_space=pl.ANY)
        vmem = pltpu.VMEM
        dma = pltpu.SemaphoreType.DMA
        flops = 2 * 6 * R * (7 * R // 3) * D
        shapes = (
            jax.ShapeDtypeStruct((R, D), bf16),
            jax.ShapeDtypeStruct((W, R), bf16),
            jax.ShapeDtypeStruct((W, R), bf16),
        )
        grads = pl.pallas_call(
            functools.partial(kernel, blocks),
            out_shape=tuple(vmem(x.shape, x.dtype) for x in shapes),
            in_specs=[hbm] * 5,
            out_specs=(hbm, hbm, hbm),
            scratch_shapes=[
                vmem((R, 2 * D), bf16), vmem((R, D), bf16),
                vmem((S, 2, 2 * D, R), bf16), vmem((S, R, R), bf16), vmem((S, R, R), bf16), vmem((S, R, R), bf16),
                vmem((S, R, R), f32), vmem((S, R, D), f32), vmem((S, R, D), f32), vmem((S, R, D), f32),
                vmem((S, R, D), f32), vmem((R, D), f32), vmem((D, R), bf16), vmem((D, R), bf16), vmem((S, 2, D, R), f32),
                vmem((R, D), f32), vmem((R, D), bf16), vmem((2, W, R), bf16),
                vmem((S, 2, 2, W, R), bf16), vmem((S, 2, 2, W, R), bf16),
                vmem((S, 2, W, R), bf16), vmem((S, 2, W, R), bf16),
                vmem((S - 1, 2, W, R), bf16), vmem((S - 1, 2, W, R), bf16),
                pltpu.SMEM((16,), jnp.int32), dma((5,)), dma((3,)),
                dma, dma((S - 1, 2, PARTS)), dma, dma((2, PARTS)), dma, dma((S - 1, 2, PARTS)),
                dma, dma((S, 2, PARTS)), dma, dma((S, 2, PARTS)),
                dma, dma((S - 1, 2, PIECES)), dma, dma((2, PIECES)), dma, dma((S - 1, 2, PIECES)), dma, dma((S, 2, PIECES)),
            ],
            compiler_params=pltpu.CompilerParams(
                collective_id=0, has_side_effects=True, vmem_limit_bytes=60 * 2**20,
            ),
            cost_estimate=pl.CostEstimate(flops=flops, bytes_accessed=4 * R * D * 2, transcendentals=R * R * 3),
        )(doc_lengths, queries, key_rows.T, value_rows.T, out_grad)
        query_grad, key_grad, value_grad = pl.pallas_call(
            hand_over, out_shape=shapes, in_specs=[hbm] * 3, out_specs=(hbm,) * 3, scratch_shapes=[dma((3,))],
            compiler_params=pltpu.CompilerParams(vmem_limit_bytes=2 * 2**20),
        )(*grads)
        return query_grad, key_grad.T, value_grad.T

    specs = (P("blk", "head"),) * 4 + (P(),)
    return jax.shard_map(shards, mesh=mesh, in_specs=specs, out_specs=specs[:3], check_vma=False)
```
